32 devices in a mesh: gx: 4 (over y, x), gy: 4 (over z), gz: 2 (over core).
Axes of the slice: x: 2, y: 2, z: 4, core: 2. Of those that a mesh axis runs over, the one named last changes fastest.
Arguments:
- labels: int32 [128, 128, 1024], P('gx', 'gy', 'gz'), may hold values from 0 to 2
- conduct_scale: float32 [128, 128, 1024], P('gx', 'gy', 'gz'), may hold values from 0.3 to 3
- phase_sigma: float32 [3], replicated, may hold values from 0.2 to 5
- source: float32 [128, 128, 1024], P('gx', 'gy', 'gz'), may hold values from -6 to 6
- potential_in: float32 [128, 128, 1024], P('gx', 'gy', 'gz'), may hold values from -6 to 6
- site_voxel: int32 [32768], P(('gx', 'gy', 'gz')), may hold values from 0 to 524287
- site_owner: int32 [32768], P(('gx', 'gy', 'gz')), may hold values from 0 to 31, as said below
- site_pore: int32 [32768], P(('gx', 'gy', 'gz')), may hold values from 0 to 511
- site_live: int32 [32768], P(('gx', 'gy', 'gz')), may hold values 0 or 1
- site_rate: float32 [32768], P(('gx', 'gy', 'gz')), may hold values from 0.05 to 0.5
- tile_press_in: float32 [2, 32768], P(None, ('gx', 'gy', 'gz')), may hold values from 0.05 to 1
- throat_nbr: int32 [8, 16384], P(None, ('gx', 'gy', 'gz')), may hold values from 0 to 16383, as said below
- throat_count: int32 [16384], P(('gx', 'gy', 'gz')), may hold values from 1 to 8
- throat_weight: float32 [8, 16384], P(None, ('gx', 'gy', 'gz')), may hold values from 0.2 to 5
- pore_exchange: float32 [16384], P(('gx', 'gy', 'gz')), may hold values from 0.1 to 1
- pore_press_in: float32 [2, 16384], P(None, ('gx', 'gy', 'gz')), may hold values from 0.1 to 1
Outputs:
- potential: float32 [128, 128, 1024], P('gx', 'gy', 'gz')
- pore_press: float32 [2, 16384], P(None, ('gx', 'gy', 'gz'))
- tile_press: float32 [2, 32768], P(None, ('gx', 'gy', 'gz'))
The draws below stay inside these ranges and needn't reach their ends.
Inputs may be any that keep to these rules, and one draw needn't show every extreme that they name: `throat_nbr`: pore p belongs to device p // 512; each throat slot names a pore of that same device or of a device whose brick shares a face with its brick. `site_owner`: each site's owner is the device holding the site or a device whose brick shares a face with that device's brick. In the rows of one device no device other than that device is named by more than 64 rows, and some other device by exactly 64.
All inputs are finite; a program needn't handle non-finite values. No bound on the sum of `site_live` on one device may be relied on, other than what follows from the above.
Results may differ from the reference program's by a relative error of at most 0.0003.
Values sent between devices are 32-bit elements; how exact they have to be, the bound alone decides.
A program may use at most 320 MiB of HBM per device.

```python
import math
import jax
import jax.numpy as jnp
from jax import lax

CX = 32
CY = 32
CZ = 512
P_DEV = 512
TPB_DEV = 1024
THR = 8
SWEEPS_E = 4
SWEEPS_G = 2
FOREIGN = 64
NX = 128
NY = 128
NZ = 1024
P_SIZE = 16384
TPB = 32768
N_GX = 4
N_GY = 4
N_GZ = 2
DEVICES = 32


def device_coords(device):
    return (device // (N_GY * N_GZ), device // N_GZ % N_GY, device % N_GZ)


def neighbour_device(device, direction):
    coord_x, coord_y, coord_z = device_coords(device)
    step = jnp.where(direction % 2 == 0, 1, -1)
    axis_of = direction // 2
    new_x = coord_x + jnp.where(axis_of == 0, step, 0)
    new_y = coord_y + jnp.where(axis_of == 1, step, 0)
    new_z = coord_z + jnp.where(axis_of == 2, step, 0)
    valid = (new_x >= 0) & (new_x < N_GX) & (new_y >= 0) & (new_y < N_GY) & (new_z >= 0) & (new_z < N_GZ)
    target = (new_x * N_GY + new_y) * N_GZ + new_z
    return (target.astype(jnp.int32), valid)


def draw_throat_nbr(key, part):
    key_local, key_away, key_dir = jax.random.split(jax.random.fold_in(key, 11), 3)
    pore_dev = (lax.broadcasted_iota(jnp.int32, (THR, P_SIZE), 1) // P_DEV).astype(jnp.int32)
    local = jax.random.randint(key_local, (THR, P_SIZE), 0, P_DEV).astype(jnp.int32)
    away = jax.random.randint(key_away, (THR, P_SIZE), 0, 20) < 3
    direction = jax.random.randint(key_dir, (THR, P_SIZE), 0, 6).astype(jnp.int32)
    target, valid = neighbour_device(pore_dev, direction)
    device = jnp.where(away & valid, target, pore_dev)
    return (device * P_DEV + local).astype(jnp.int32)


def draw_site_owner(key, part):
    key_count, key_axis, key_perm = jax.random.split(jax.random.fold_in(key, 23), 3)
    devices = jnp.arange(DEVICES, dtype=jnp.int32)
    counts = jax.random.randint(key_count, (DEVICES, 6), 1, FOREIGN + 1).astype(jnp.int32)
    forced_axis = jax.random.randint(key_axis, (DEVICES,), 0, 3).astype(jnp.int32)
    coord_x, coord_y, coord_z = device_coords(devices)
    coord = jnp.where(forced_axis == 0, coord_x, jnp.where(forced_axis == 1, coord_y, coord_z))
    extent = jnp.where(forced_axis == 0, N_GX, jnp.where(forced_axis == 1, N_GY, N_GZ))
    forced_dir = 2 * forced_axis + jnp.where(coord < extent - 1, 0, 1)
    counts = jnp.where(jnp.arange(6, dtype=jnp.int32)[None, :] == forced_dir[:, None], FOREIGN, counts)
    perm_keys = jax.random.split(key_perm, DEVICES)
    slots = jax.vmap(lambda k: jax.random.permutation(k, TPB_DEV))(perm_keys).astype(jnp.int32)
    direction = jnp.minimum(slots // FOREIGN, 5)
    taken_count = jnp.take_along_axis(counts, direction, axis=1)
    taken = (slots < 6 * FOREIGN) & (slots % FOREIGN < taken_count)
    own = jnp.broadcast_to(devices[:, None], (DEVICES, TPB_DEV))
    target, valid = neighbour_device(own, direction)
    owner = jnp.where(taken & valid, target, own)
    return owner.reshape(-1).astype(jnp.int32)


def plant(result, own_key, smallest, high):
    longest = result.shape.index(max(result.shape))
    spots = []
    for shift in (0, 1):
        where = [jax.random.randint(jax.random.fold_in(own_key, axis), (), 0, length) for axis, length in enumerate(result.shape)]
        where[longest] = (where[longest] + shift) % result.shape[longest]
        spots.append(tuple(where))
    return result.at[spots[0]].set(smallest).at[spots[1]].set(high)


def levels(key, shape, pieces, smallest, high):
    def one(dim, parts):
        draws = jax.random.uniform(jax.random.fold_in(jax.random.fold_in(key, 6), dim), (parts,), jnp.float32, smallest / len(pieces), high / len(pieces))
        return jnp.repeat(jnp.exp(draws), shape[dim] // parts).reshape((-1,) + (1,) * (len(shape) - dim - 1))

    level = one(*pieces[0])
    for cut in pieces[1:]:
        level = level * one(*cut)
    return level


def noise(rng, dims, width, most, pieces=(), kind=jnp.bfloat16):
    loudness = levels(rng, dims, pieces, -0.22, 0.18) if pieces else 1.0
    drawn = jax.random.normal(rng, dims, jnp.float32) * width * loudness
    return jnp.minimum(jnp.maximum(drawn, -most), most).astype(kind)


def setup_inputs(seed: int = 0) -> dict:
    streams_of = jax.random.split(jax.random.key(seed), 17)
    return {
        "labels": plant(jax.random.randint(streams_of[0], (NX, NY, NZ), 0, 3), jax.random.fold_in(streams_of[0], 1), 0, 2).astype(jnp.int32),
        "conduct_scale": jnp.clip(jnp.exp(math.log(3.0) - 2.3025851 * jax.random.uniform(streams_of[1], (NX, NY, NZ), jnp.float32) ** levels(streams_of[1], (NX, NY, NZ), ((0, 4), (1, 4), (2, 2)), -0.2, 0.2)), 0.3, 3.0),
        "phase_sigma": jnp.clip(jnp.exp(jax.random.uniform(streams_of[2], (3,), jnp.float32, math.log(0.2), math.log(5.0))), 0.2, 5.0),
        "source": noise(streams_of[3], (NX, NY, NZ), 1.0, 6.0, ((0, 4), (1, 4), (2, 2)), jnp.float32),
        "potential_in": noise(streams_of[4], (NX, NY, NZ), 1.0, 6.0, ((0, 4), (1, 4), (2, 2)), jnp.float32),
        "site_voxel": plant(jax.random.randint(streams_of[5], (TPB,), 0, CX * CY * CZ), jax.random.fold_in(streams_of[5], 1), 0, (CX * CY * CZ) - 1).astype(jnp.int32),
        "site_owner": draw_site_owner(jax.random.fold_in(streams_of[16], 71), 0),
        "site_pore": plant(jax.random.randint(streams_of[7], (TPB,), 0, P_DEV), jax.random.fold_in(streams_of[7], 1), 0, P_DEV - 1).astype(jnp.int32),
        "site_live": plant((jax.random.randint(streams_of[8], (TPB,), 0, 4) < 3).astype(jnp.int32), jax.random.fold_in(streams_of[8], 1), 0, 1),
        "site_rate": jnp.clip(jnp.exp(math.log(0.5) - 2.3025851 * jax.random.uniform(streams_of[9], (TPB,), jnp.float32) ** levels(streams_of[9], (TPB,), ((0, 32),), -0.2, 0.2)), 0.05, 0.5),
        "tile_press_in": jnp.clip(jnp.exp(math.log(1.0) - 2.9957323 * jax.random.uniform(streams_of[10], (2, TPB), jnp.float32) ** levels(streams_of[10], (2, TPB), ((1, 32),), -0.2, 0.2)), 0.05, 1.0),
        "throat_nbr": draw_throat_nbr(jax.random.fold_in(streams_of[16], 71), 0),
        "throat_count": plant(jax.random.randint(streams_of[12], (P_SIZE,), 1, THR + 1), jax.random.fold_in(streams_of[12], 1), 1, THR).astype(jnp.int32),
        "throat_weight": jnp.clip(jnp.exp(math.log(5.0) - 3.218876 * jax.random.uniform(streams_of[13], (THR, P_SIZE), jnp.float32) ** levels(streams_of[13], (THR, P_SIZE), ((1, 32),), -0.2, 0.2)), 0.2, 5.0),
        "pore_exchange": jnp.clip(jnp.exp(math.log(1.0) - 2.3025851 * jax.random.uniform(streams_of[14], (P_SIZE,), jnp.float32) ** levels(streams_of[14], (P_SIZE,), ((0, 32),), -0.2, 0.2)), 0.1, 1.0),
        "pore_press_in": jnp.clip(jnp.exp(math.log(1.0) - 2.3025851 * jax.random.uniform(streams_of[15], (2, P_SIZE), jnp.float32) ** levels(streams_of[15], (2, P_SIZE), ((1, 32),), -0.2, 0.2)), 0.1, 1.0),
    }


REACT = 0.1
DK_A = 2.0
DK_B = 0.7
DIFF_M = 1.0
BATH_A = 1.0
BATH_B = 0.2
CURRENT_SCALE = 0.25


def conductivity(labels, conduct_scale, phase_sigma):
    table = jnp.where(labels == 0, phase_sigma[0], jnp.where(labels == 1, phase_sigma[1], phase_sigma[2]))
    return conduct_scale * table


def beside(arr):
    return (arr[2:, 1:-1, 1:-1], arr[:-2, 1:-1, 1:-1], arr[1:-1, 2:, 1:-1],
            arr[1:-1, :-2, 1:-1], arr[1:-1, 1:-1, 2:], arr[1:-1, 1:-1, :-2])


def relax(phi_pad, sig_pad, source):
    centre = sig_pad[1:-1, 1:-1, 1:-1]
    numer = source
    denom = jnp.zeros_like(source) + REACT
    for near_phi, near_sig in zip(beside(phi_pad), beside(sig_pad)):
        face = 0.5 * (centre + near_sig)
        numer = numer + face * near_phi
        denom = denom + face
    return jnp.where(centre > 0.0, numer / denom, 0.0)


def butler(volt, site_rate, tile_press_in, site_live):
    eta = volt - 0.5 * jnp.log(tile_press_in[1] / tile_press_in[0])
    return site_live.astype(site_rate.dtype) * site_rate * (jnp.exp(0.6 * eta) - jnp.exp(-0.4 * eta))


def diffuse(own, near, throat_count, throat_weight, pore_exchange, pore_current):
    slot = lax.broadcasted_iota(jnp.int32, throat_weight.shape, 0)
    masked = jnp.where(slot < throat_count[None, :], throat_weight, 0.0)
    wsum = jnp.sum(masked, axis=0)
    sum_a = jnp.sum(masked * near[0], axis=0)
    sum_b = jnp.sum(masked * near[1], axis=0)
    mag_a = jnp.abs(own[0])
    mag_b = jnp.abs(own[1])
    total = mag_a + mag_b + 1.0
    diff_a = DK_A / (1.0 + DK_A / DIFF_M * mag_b / total)
    diff_b = DK_B / (1.0 + DK_B / DIFF_M * mag_a / total)
    new_a = (diff_a * sum_a + pore_exchange * BATH_A - CURRENT_SCALE * pore_current) / (diff_a * wsum + pore_exchange)
    new_b = (diff_b * sum_b + pore_exchange * BATH_B + CURRENT_SCALE * pore_current) / (diff_b * wsum + pore_exchange)
    return jnp.stack([new_a, new_b])


def reference(labels, conduct_scale, phase_sigma, source, potential_in, site_voxel, site_owner, site_pore,
              site_live, site_rate, tile_press_in, throat_nbr, throat_count, throat_weight, pore_exchange,
              pore_press_in):
    sigma = conductivity(labels, conduct_scale, phase_sigma)
    sig_pad = jnp.pad(sigma, 1)
    phi = potential_in
    for sweep in range(SWEEPS_E):
        phi = relax(jnp.pad(phi, 1), sig_pad, source)
    site_ids = jnp.arange(TPB, dtype=jnp.int32)
    device = site_ids // TPB_DEV
    brick_x = device // (N_GY * N_GZ)
    brick_y = (device // N_GZ) % N_GY
    brick_z = device % N_GZ
    local_x = site_voxel // (CY * CZ)
    local_y = (site_voxel // CZ) % CY
    local_z = site_voxel % CZ
    volt = phi[brick_x * CX + local_x, brick_y * CY + local_y, brick_z * CZ + local_z]
    current = butler(volt, site_rate, tile_press_in, site_live)
    pore_gid = (site_owner * P_DEV + site_pore).astype(jnp.int32)
    pore_current = jnp.zeros((P_SIZE,), current.dtype).at[pore_gid].add(current)
    press = pore_press_in
    for sweep in range(SWEEPS_G):
        near = press[:, throat_nbr]
        press = diffuse(press, near, throat_count, throat_weight, pore_exchange, pore_current)
    tile_press = press[:, pore_gid] * site_live.astype(press.dtype)[None, :]
    return phi, press, tile_press
```

```python
import functools

import jax
import jax.numpy as jnp
from jax import lax
from jax.experimental import pallas as pl
from jax.experimental.pallas import tpu as pltpu
from jax.sharding import PartitionSpec as P

SWEEPS_E = 4
SWEEPS_G = 2
REACT = 0.1
DK_A = 2.0
DK_B = 0.7
DIFF_M = 1.0
BATH_A = 1.0
BATH_B = 0.2
CURRENT_SCALE = 0.25

LANES = 128
CHUNKS = 4
ORDER = (0, 3, 1, 2)
SLOTS = 7
MESH = pl.DeviceIdType.MESH


def up_z(v, after):
    ext = jnp.concatenate([v, after], axis=1)
    return pltpu.roll(ext, ext.shape[1] - 1, 1)[:, : v.shape[1]]


def down_z(v, before):
    ext = jnp.concatenate([before, v], axis=1)
    return pltpu.roll(ext, 1, 1)[:, before.shape[1] :]


def up_y(v, row, is_last):
    return jnp.where(is_last, row, pltpu.roll(v, v.shape[0] - 1, 0))


def down_y(v, row, is_first):
    return jnp.where(is_first, row, pltpu.roll(v, 1, 0))


def kernel(
    sizes,
    table_ref,
    lab_hbm,
    cs_hbm,
    src_hbm,
    phi_hbm,
    voxel_ref,
    owner_ref,
    spore_ref,
    live_ref,
    rate_ref,
    tpress_ref,
    nbr_ref,
    count_ref,
    weight_ref,
    exch_ref,
    press_ref,
    phi_out,
    press_out,
    tile_out,
    lab,
    cs,
    src,
    sig,
    phi0,
    phi1,
    phi2,
    phi3,
    fin,
    gxf,
    gyf,
    gzf,
    inv,
    ylo,
    yhi,
    ysend_lo,
    ysend_hi,
    zlo,
    zhi,
    onehot,
    tab0,
    tab1,
    tab2,
    bucket,
    arrived,
    load_sem,
    out_sem,
    xs_sem,
    xr_sem,
    ys_sem,
    yr_sem,
    zs_sem,
    zr_sem,
    ps_sem,
    pr_sem,
):
    size_x, size_y, size_z = sizes
    nx, ny, nz = src.shape
    nc = nx // CHUNKS
    pores = press_ref.shape[1]
    segs = pores // LANES
    ix, iy, iz = (lax.axis_index("gx"), lax.axis_index("gy"), lax.axis_index("gz"))

    axes = (("gx", ix, size_x), ("gy", iy, size_y), ("gz", iz, size_z))
    there = []
    where_to = []
    for name, at, size in axes:
        there += [at > 0, at < size - 1]
        where_to += [{name: at - 1}, {name: at + 1}]

    def load(which, chunk):
        rows = pl.ds(chunk * nc, nc)
        far, near = ((lab_hbm, lab), (cs_hbm, cs), (phi_hbm, phi0), (src_hbm, src))[which]
        inner = pl.ds(1 + chunk * nc, nc) if which == 2 else rows
        return pltpu.make_async_copy(far.at[rows], near.at[inner], load_sem.at[which, chunk])

    for part in ((0, 1), (2,), (3,)):
        for chunk in ORDER:
            for which in part:
                load(which, chunk).start()

    barrier = pltpu.get_barrier_semaphore()
    total = jnp.int32(0)
    for k in range(6):
        total = total + there[k].astype(jnp.int32)

        @pl.when(there[k])
        def _():
            pl.semaphore_signal(barrier, inc=1, device_id=where_to[k], device_id_type=MESH)

    fields = (sig, phi0, phi1, phi2, phi3)

    def x_copy(e, side):
        field = fields[e]
        return pltpu.make_async_remote_copy(
            src_ref=field.at[1 if side == 0 else nx],
            dst_ref=field.at[nx + 1 if side == 0 else 0],
            send_sem=xs_sem.at[e, side],
            recv_sem=xr_sem.at[e, 1 - side],
            device_id=where_to[side],
            device_id_type=MESH,
        )

    def y_copy(e, side, chunk):
        rows = pl.ds(chunk * nc, nc)
        return pltpu.make_async_remote_copy(
            src_ref=(ysend_lo if side == 0 else ysend_hi).at[e, rows],
            dst_ref=(yhi if side == 0 else ylo).at[e, rows],
            send_sem=ys_sem.at[e, side, chunk],
            recv_sem=yr_sem.at[e, 1 - side, chunk],
            device_id=where_to[2 + side],
            device_id_type=MESH,
        )

    def z_copy(e, side, chunk):
        return pltpu.make_async_remote_copy(
            src_ref=fields[e].at[
                pl.ds(1 + chunk * nc, nc), :, pl.ds(0 if side == 0 else nz - LANES, LANES)
            ],
            dst_ref=(zhi if side == 0 else zlo).at[e, pl.ds(chunk * nc, nc)],
            send_sem=zs_sem.at[e, side, chunk],
            recv_sem=zr_sem.at[e, 1 - side, chunk],
            device_id=where_to[4 + side],
            device_id_type=MESH,
        )

    tabs = (tab0, tab1, tab2)

    def p_copy(e, k):
        opposite = 1 + (k ^ 1)
        return pltpu.make_async_remote_copy(
            src_ref=tabs[e].at[0] if e < 3 else bucket.at[1 + k],
            dst_ref=tabs[e].at[opposite] if e < 3 else arrived.at[opposite],
            send_sem=ps_sem.at[e, k],
            recv_sem=pr_sem.at[e, k ^ 1],
            device_id=where_to[k],
            device_id_type=MESH,
        )


    def send_faces(e, chunk):
        if chunk == 0:

            @pl.when(there[0])
            def _():
                x_copy(e, 0).start()

        if chunk == CHUNKS - 1:

            @pl.when(there[1])
            def _():
                x_copy(e, 1).start()

        for side in (0, 1):

            @pl.when(there[2 + side])
            def _():
                y_copy(e, side, chunk).start()

            @pl.when(there[4 + side])
            def _():
                z_copy(e, side, chunk).start()

    def await_faces(e, chunk):
        if chunk == 0:

            @pl.when(there[0])
            def _():
                x_copy(e, 1).wait_recv()

        if chunk == CHUNKS - 1:

            @pl.when(there[1])
            def _():
                x_copy(e, 0).wait_recv()

        for side in (0, 1):

            @pl.when(there[2 + side])
            def _():
                y_copy(e, 1 - side, chunk).wait_recv()

            @pl.when(there[4 + side])
            def _():
                z_copy(e, 1 - side, chunk).wait_recv()

    def send_pores(e):
        for k in range(6):

            @pl.when(there[k])
            def _():
                p_copy(e, k).start()

    def await_pores(e):
        for k in range(6):

            @pl.when(there[k])
            def _():
                p_copy(e, k ^ 1).wait_recv()

    for side, (xat, ybuf, zbuf) in enumerate(((0, ylo, zlo), (nx + 1, yhi, zhi))):

        @pl.when(jnp.logical_not(there[side]))
        def _():
            for field in fields:
                field[xat] = jnp.zeros((ny, nz), jnp.float32)

        @pl.when(jnp.logical_not(there[2 + side]))
        def _():
            ybuf[...] = jnp.zeros(ybuf.shape, jnp.float32)

        @pl.when(jnp.logical_not(there[4 + side]))
        def _():
            for e in range(5):

                def clear(i, carry):
                    zbuf[e, i] = jnp.zeros((ny, LANES), jnp.float32)
                    return carry

                lax.fori_loop(0, nx, clear, 0)

    for k in range(6):

        @pl.when(jnp.logical_not(there[k]))
        def _():
            for tab in tabs:
                tab[1 + k] = jnp.zeros((2, pores), jnp.float32)
            arrived[1 + k] = jnp.zeros((1, pores), jnp.float32)

    tab0[0] = press_ref[...]

    pl.semaphore_wait(barrier, total)
    send_pores(0)

    s0, s1, s2 = (table_ref[0], table_ref[1], table_ref[2])
    for chunk in ORDER:
        load(0, chunk).wait()
        load(1, chunk).wait()

        def conductivity(i, carry):
            kind = lab[i]
            value = cs[i] * jnp.where(kind == 0, s0, jnp.where(kind == 1, s1, s2))
            sig[i + 1] = value
            ysend_lo[0, i] = value[0:1]
            ysend_hi[0, i] = value[ny - 1 : ny]
            return carry

        lax.fori_loop(chunk * nc, (chunk + 1) * nc, conductivity, 0)
        send_faces(0, chunk)
    for chunk in ORDER:
        load(2, chunk).wait()

        def pack(i, carry):
            ysend_lo[1, i] = phi0[i + 1, 0:1]
            ysend_hi[1, i] = phi0[i + 1, ny - 1 : ny]
            return carry

        lax.fori_loop(chunk * nc, (chunk + 1) * nc, pack, 0)
        send_faces(1, chunk)

    own = (ix * size_y + iy) * size_z + iz
    bits = pores.bit_length() - 1
    lane_bits = LANES.bit_length() - 1

    def place(device, local):
        delta = device - own
        slot = jnp.zeros(delta.shape, jnp.int32)
        for k, step in enumerate(
            (-size_y * size_z, size_y * size_z, -size_z, size_z, -1, 1)
        ):
            slot = jnp.where(delta == step, k + 1, slot)
        return slot, slot * segs + (local >> lane_bits), local & (LANES - 1)

    nbr = nbr_ref[...]
    _, near_key, near_lane = place(nbr >> bits, nbr & (pores - 1))
    site_pore = spore_ref[...]
    site_slot, site_key, site_lane = place(owner_ref[...], site_pore)
    live = live_ref[...].astype(jnp.float32)
    slot_no = lax.broadcasted_iota(jnp.int32, weight_ref.shape, 0)
    masked = jnp.where(slot_no < count_ref[...], weight_ref[...], 0.0)
    wsum = jnp.sum(masked, axis=0, keepdims=True)
    exch = exch_ref[...]
    pore_no = lax.broadcasted_iota(jnp.int32, (pores, LANES), 0)
    site_rows = site_pore.shape[0]
    for r in range(site_rows):
        hit = jnp.where(pore_no == site_pore[r : r + 1], 1.0, 0.0)
        onehot[:, r * LANES : (r + 1) * LANES] = hit.astype(jnp.bfloat16)

    y_no = lax.broadcasted_iota(jnp.int32, (ny, nz), 0)
    y_first = y_no == 0
    y_last = y_no == ny - 1

    for sweep in range(SWEEPS_E):
        old = fields[1 + sweep]
        last = sweep == SWEEPS_E - 1
        e = 1 + sweep
        for chunk in ORDER:
            if sweep == 0:
                await_faces(0, chunk)
                load(3, chunk).wait()
            await_faces(e, chunk)

            def relax(i, carry):
                phi = old[i + 1]
                if sweep == 0:
                    s = sig[i + 1]
                    g_below = 0.5 * (sig[i] + s)
                    g_above = 0.5 * (s + sig[i + 2])
                    gy = 0.5 * (s + up_y(s, yhi[0, i], y_last))
                    gz = 0.5 * (s + up_z(s, zhi[0, i]))
                    y_low = 0.5 * (ylo[0, i] + s[0:1])
                    gxf[i] = g_below
                    gxf[i + 1] = g_above
                    gyf[i] = gy
                    gzf[i] = gz
                    z_low = 0.5 * (zlo[0, i] + pltpu.roll(s[:, :LANES], LANES - 1, 1))
                    ylo[0, i] = y_low
                    zlo[0, i] = z_low
                    denom = (
                        REACT
                        + g_below
                        + g_above
                        + gy
                        + down_y(gy, y_low, y_first)
                        + gz
                        + down_z(gz, z_low)
                    )
                    scale = jnp.where(s > 0.0, 1.0 / denom, 0.0)
                    inv[i] = scale
                else:
                    g_below = gxf[i]
                    g_above = gxf[i + 1]
                    gy = gyf[i]
                    gz = gzf[i]
                    y_low = ylo[0, i]
                    z_low = zlo[0, i]
                    scale = inv[i]
                numer = (
                    src[i]
                    + g_below * old[i]
                    + g_above * old[i + 2]
                    + gy * up_y(phi, yhi[e, i], y_last)
                    + down_y(gy * phi, y_low * ylo[e, i], y_first)
                    + gz * up_z(phi, zhi[e, i])
                    + down_z(gz * phi, z_low * zlo[e, i])
                )
                value = numer * scale
                if last:
                    fin[i] = value
                else:
                    fields[e + 1][i + 1] = value
                    ysend_lo[e + 1, i] = value[0:1]
                    ysend_hi[e + 1, i] = value[ny - 1 : ny]
                return carry

            lax.fori_loop(chunk * nc, (chunk + 1) * nc, relax, 0)
            if last:
                rows = pl.ds(chunk * nc, nc)
                pltpu.make_async_copy(fin.at[rows], phi_out.at[rows], out_sem.at[chunk]).start()
            else:
                send_faces(e + 1, chunk)

    voxel = voxel_ref[...]
    y_bits, z_bits = (ny.bit_length() - 1, nz.bit_length() - 1)
    vz = voxel & (nz - 1)
    vy = (voxel >> z_bits) & (ny - 1)
    vx = voxel >> (z_bits + y_bits)
    y_tiles, z_tiles = (ny // 8, nz // LANES)
    tile_no = (vx * y_tiles + (vy >> 3)) * z_tiles + (vz >> lane_bits)
    sub = lax.broadcasted_iota(jnp.int32, (8, LANES), 0)

    def spread(a, r):
        return jnp.broadcast_to(a[r : r + 1], (8, LANES))

    tile_rows = [spread(tile_no, r) for r in range(site_rows)]
    lane_rows = [spread(vz & (LANES - 1), r) for r in range(site_rows)]

    def pick(i, accs):
        accs = list(accs)
        for ty in range(y_tiles):
            for tz in range(z_tiles):
                block = fin[i, ty * 8 : ty * 8 + 8, tz * LANES : (tz + 1) * LANES]
                here = (i * y_tiles + ty) * z_tiles + tz
                for r in range(site_rows):
                    got = jnp.take_along_axis(block, lane_rows[r], axis=1)
                    accs[r] = jnp.where(tile_rows[r] == here, got, accs[r])
        return tuple(accs)

    zero = jnp.zeros((8, LANES), jnp.float32)
    accs = lax.fori_loop(0, nx, pick, (zero,) * site_rows)
    volt = jnp.concatenate(
        [
            jnp.sum(jnp.where(sub == spread(vy & 7, r), accs[r], 0.0), axis=0, keepdims=True)
            for r in range(site_rows)
        ],
        axis=0,
    )
    ratio = tpress_ref[1:2, :] / tpress_ref[0:1, :]
    ratio = jnp.concatenate(
        [ratio[:, r * LANES : (r + 1) * LANES] for r in range(site_rows)], axis=0
    )
    eta = volt - 0.5 * jnp.log(ratio)
    current = live * rate_ref[...] * (jnp.exp(0.6 * eta) - jnp.exp(-0.4 * eta))

    spread_current = jnp.concatenate(
        [
            jnp.where(sub == spread(site_slot, r), spread(current, r), 0.0)
            for r in range(site_rows)
        ],
        axis=1,
    )
    high = spread_current.astype(jnp.bfloat16).astype(jnp.float32)
    rest = spread_current - high
    middle = rest.astype(jnp.bfloat16).astype(jnp.float32)
    low = rest - middle
    parts = jnp.concatenate([high, middle, low, jnp.zeros_like(low)], axis=0).astype(jnp.bfloat16)
    sums = lax.dot_general(
        parts, onehot[...], (((1,), (1,)), ((), ())), preferred_element_type=jnp.float32
    )
    sums = sums[0:8] + sums[8:16] + sums[16:24]
    for k in range(SLOTS):
        bucket[k] = sums[k : k + 1]
    send_pores(3)

    def look_up(tab, key, lane):
        found = [zero, zero]
        for k in range(SLOTS):
            for seg in range(segs):
                hit = key == k * segs + seg
                for c in range(2):
                    row = tab[k, c : c + 1, seg * LANES : (seg + 1) * LANES]
                    got = jnp.take_along_axis(jnp.broadcast_to(row, (8, LANES)), lane, axis=1)
                    found[c] = jnp.where(hit, got, found[c])
        return found

    def diffuse(tab):
        near = ([], [])
        for j in range(segs):
            cut = slice(j * LANES, (j + 1) * LANES)
            a, b = look_up(tab, near_key[:, cut], near_lane[:, cut])
            near[0].append(a)
            near[1].append(b)
        sum_a = jnp.sum(masked * jnp.concatenate(near[0], axis=1), axis=0, keepdims=True)
        sum_b = jnp.sum(masked * jnp.concatenate(near[1], axis=1), axis=0, keepdims=True)
        mag_a = jnp.abs(tab[0, 0:1])
        mag_b = jnp.abs(tab[0, 1:2])
        size = mag_a + mag_b + 1.0
        diff_a = DK_A / (1.0 + DK_A / DIFF_M * mag_b / size)
        diff_b = DK_B / (1.0 + DK_B / DIFF_M * mag_a / size)
        return (
            diff_a * sum_a + exch * BATH_A,
            diff_b * sum_b + exch * BATH_B,
            diff_a * wsum + exch,
            diff_b * wsum + exch,
        )

    await_pores(0)
    drawn = None
    for sweep in range(SWEEPS_G):
        top_a, top_b, bottom_a, bottom_b = diffuse(tabs[sweep])
        if sweep == 0:
            await_pores(3)
            drawn = bucket[0]
            for k in range(6):
                drawn = drawn + arrived[1 + k]
            drawn = CURRENT_SCALE * drawn
        new_a = (top_a - drawn) / bottom_a
        new_b = (top_b + drawn) / bottom_b
        tabs[sweep + 1][0, 0:1] = new_a
        tabs[sweep + 1][0, 1:2] = new_b
        send_pores(sweep + 1)
        if sweep == SWEEPS_G - 1:
            press_out[0:1, :] = new_a
            press_out[1:2, :] = new_b
        await_pores(sweep + 1)

    found = look_up(tabs[SWEEPS_G], site_key, site_lane)
    for c in range(2):
        values = found[c] * live
        for r in range(site_rows):
            tile_out[c : c + 1, r * LANES : (r + 1) * LANES] = values[r : r + 1]

    for e in range(5):
        for side in (0, 1):

            @pl.when(there[side])
            def _():
                x_copy(e, side).wait_send()

            for chunk in range(CHUNKS):

                @pl.when(there[2 + side])
                def _():
                    y_copy(e, side, chunk).wait_send()

                @pl.when(there[4 + side])
                def _():
                    z_copy(e, side, chunk).wait_send()

    for e in range(4):
        for k in range(6):

            @pl.when(there[k])
            def _():
                p_copy(e, k).wait_send()

    for chunk in range(CHUNKS):
        rows = pl.ds(chunk * nc, nc)
        pltpu.make_async_copy(fin.at[rows], phi_out.at[rows], out_sem.at[chunk]).wait()


def body(
    labels,
    conduct_scale,
    phase_sigma,
    source,
    potential_in,
    site_voxel,
    site_owner,
    site_pore,
    site_live,
    site_rate,
    tile_press_in,
    throat_nbr,
    throat_count,
    throat_weight,
    pore_exchange,
    pore_press_in,
):
    sizes = (lax.axis_size("gx"), lax.axis_size("gy"), lax.axis_size("gz"))
    nx, ny, nz = source.shape
    pores = pore_exchange.shape[0]
    sites = site_voxel.shape[0]
    f32 = jnp.float32

    def brick(extra=0):
        return pltpu.VMEM((nx + extra, ny, nz), f32)

    dma = pltpu.SemaphoreType.DMA
    any_spec = pl.BlockSpec(memory_space=pl.ANY)
    vmem = pl.BlockSpec(memory_space=pltpu.VMEM)
    by_row = (sites // LANES, LANES)
    return pl.pallas_call(
        functools.partial(kernel, sizes),
        out_shape=(
            jax.ShapeDtypeStruct((nx, ny, nz), f32),
            jax.ShapeDtypeStruct((2, pores), f32),
            jax.ShapeDtypeStruct((2, sites), f32),
        ),
        in_specs=[pl.BlockSpec(memory_space=pltpu.SMEM)] + [any_spec] * 4 + [vmem] * 11,
        out_specs=(any_spec, vmem, vmem),
        scratch_shapes=[
            pltpu.VMEM((nx, ny, nz), jnp.int32),
            brick(),
            brick(),
            brick(2),
            brick(2),
            brick(2),
            brick(2),
            brick(2),
            brick(),
            brick(1),
            brick(),
            brick(),
            brick(),
            pltpu.VMEM((5, nx, 1, nz), f32),
            pltpu.VMEM((5, nx, 1, nz), f32),
            pltpu.VMEM((5, nx, 1, nz), f32),
            pltpu.VMEM((5, nx, 1, nz), f32),
            pltpu.VMEM((5, nx, ny, LANES), f32),
            pltpu.VMEM((5, nx, ny, LANES), f32),
            pltpu.VMEM((pores, sites), jnp.bfloat16),
            pltpu.VMEM((SLOTS, 2, pores), f32),
            pltpu.VMEM((SLOTS, 2, pores), f32),
            pltpu.VMEM((SLOTS, 2, pores), f32),
            pltpu.VMEM((SLOTS, 1, pores), f32),
            pltpu.VMEM((SLOTS, 1, pores), f32),
            dma((4, CHUNKS)),
            dma((CHUNKS,)),
            dma((5, 2)),
            dma((5, 2)),
            dma((5, 2, CHUNKS)),
            dma((5, 2, CHUNKS)),
            dma((5, 2, CHUNKS)),
            dma((5, 2, CHUNKS)),
            dma((4, 6)),
            dma((4, 6)),
        ],
        compiler_params=pltpu.CompilerParams(
            collective_id=0, has_side_effects=True, vmem_limit_bytes=58 * 1024 * 1024
        ),
    )(
        phase_sigma,
        labels,
        conduct_scale,
        source,
        potential_in,
        site_voxel.reshape(by_row),
        site_owner.reshape(by_row),
        site_pore.reshape(by_row),
        site_live.reshape(by_row),
        site_rate.reshape(by_row),
        tile_press_in,
        throat_nbr,
        throat_count.reshape(1, pores),
        throat_weight,
        pore_exchange.reshape(1, pores),
        pore_press_in,
    )


def solution(mesh):
    return jax.shard_map(
        body,
        mesh=mesh,
        in_specs=(
            P("gx", "gy", "gz"),
            P("gx", "gy", "gz"),
            P(),
            P("gx", "gy", "gz"),
            P("gx", "gy", "gz"),
            P(("gx", "gy", "gz")),
            P(("gx", "gy", "gz")),
            P(("gx", "gy", "gz")),
            P(("gx", "gy", "gz")),
            P(("gx", "gy", "gz")),
            P(None, ("gx", "gy", "gz")),
            P(None, ("gx", "gy", "gz")),
            P(("gx", "gy", "gz")),
            P(None, ("gx", "gy", "gz")),
            P(("gx", "gy", "gz")),
            P(None, ("gx", "gy", "gz")),
        ),
        out_specs=(P("gx", "gy", "gz"), P(None, ("gx", "gy", "gz")), P(None, ("gx", "gy", "gz"))),
        check_vma=False,
    )
```

```python
import functools

import jax
import jax.numpy as jnp
from jax import lax
from jax.experimental import pallas as pl
from jax.experimental.pallas import tpu as pltpu
from jax.sharding import PartitionSpec as P

SWEEPS_E = 4
SWEEPS_G = 2
REACT = 0.1
DK_A = 2.0
DK_B = 0.7
DIFF_M = 1.0
BATH_A = 1.0
BATH_B = 0.2
CURRENT_SCALE = 0.25

LANES = 128
CHUNKS = 4
ORDER = (0, 3, 1, 2)
SLOTS = 7
MESH = pl.DeviceIdType.MESH


TOP = 8


def up_z(blocks, after, is_last):
    turned = [pltpu.roll(v, LANES - 1, 1) for v in [*blocks, after]]
    return [jnp.where(is_last, b, a) for a, b in zip(turned[:-1], turned[1:])]


def down_z(blocks, before, is_first):
    turned = [pltpu.roll(v, 1, 1) for v in [before, *blocks]]
    return [jnp.where(is_first, a, b) for a, b in zip(turned[:-1], turned[1:])]


def kernel(
    sizes,
    table_ref,
    lab_hbm,
    cs_hbm,
    src_hbm,
    phi_hbm,
    voxel_ref,
    owner_ref,
    spore_ref,
    live_ref,
    rate_ref,
    tpress_ref,
    nbr_ref,
    count_ref,
    weight_ref,
    exch_ref,
    press_ref,
    phi_out,
    press_out,
    tile_out,
    lab,
    cs,
    src,
    sig,
    phi0,
    phi1,
    phi2,
    phi3,
    fin,
    gxf,
    gyf,
    gzf,
    glow,
    inv,
    zlo,
    zhi,
    onehot,
    tab0,
    tab1,
    tab2,
    bucket,
    arrived,
    load_sem,
    out_sem,
    xs_sem,
    xr_sem,
    ys_sem,
    yr_sem,
    zs_sem,
    zr_sem,
    ps_sem,
    pr_sem,
):
    size_x, size_y, size_z = sizes
    nx, zts, ny, _ = src.shape
    nz = zts * LANES
    nc = nx // CHUNKS
    inside = pl.ds(TOP, ny)
    pores = press_ref.shape[1]
    segs = pores // LANES
    ix, iy, iz = (lax.axis_index("gx"), lax.axis_index("gy"), lax.axis_index("gz"))

    axes = (("gx", ix, size_x), ("gy", iy, size_y), ("gz", iz, size_z))
    there = []
    where_to = []
    for name, at, size in axes:
        there += [at > 0, at < size - 1]
        where_to += [{name: at - 1}, {name: at + 1}]

    def load(which, chunk, zt):
        rows = pl.ds(chunk * nc, nc)
        far, near = ((lab_hbm, lab), (cs_hbm, cs), (phi_hbm, phi0), (src_hbm, src))[which]
        if which == 2:
            near = near.at[pl.ds(1 + chunk * nc, nc), zt, inside]
        else:
            near = near.at[rows, zt]
        return pltpu.make_async_copy(
            far.at[rows, :, pl.ds(zt * LANES, LANES)], near, load_sem.at[which, chunk, zt]
        )

    def unload(chunk, zt):
        rows = pl.ds(chunk * nc, nc)
        return pltpu.make_async_copy(
            fin.at[rows, zt],
            phi_out.at[rows, :, pl.ds(zt * LANES, LANES)],
            out_sem.at[chunk, zt],
        )

    for part in ((0, 1), (2,), (3,)):
        for chunk in ORDER:
            for which in part:
                for zt in range(zts):
                    load(which, chunk, zt).start()

    barrier = pltpu.get_barrier_semaphore()
    total = jnp.int32(0)
    for k in range(6):
        total = total + there[k].astype(jnp.int32)

        @pl.when(there[k])
        def _():
            pl.semaphore_signal(barrier, inc=1, device_id=where_to[k], device_id_type=MESH)

    fields = (sig, phi0, phi1, phi2, phi3)

    def x_copy(e, side):
        field = fields[e]
        return pltpu.make_async_remote_copy(
            src_ref=field.at[1 if side == 0 else nx, :, inside],
            dst_ref=field.at[nx + 1 if side == 0 else 0, :, inside],
            send_sem=xs_sem.at[e, side],
            recv_sem=xr_sem.at[e, 1 - side],
            device_id=where_to[side],
            device_id_type=MESH,
        )

    def y_copy(e, side, chunk):
        rows = pl.ds(1 + chunk * nc, nc)
        first, final = (TOP, TOP + ny - 1)
        return pltpu.make_async_remote_copy(
            src_ref=fields[e].at[rows, :, pl.ds(first if side == 0 else final, 1)],
            dst_ref=fields[e].at[rows, :, pl.ds(final + 1 if side == 0 else first - 1, 1)],
            send_sem=ys_sem.at[e, side, chunk],
            recv_sem=yr_sem.at[e, 1 - side, chunk],
            device_id=where_to[2 + side],
            device_id_type=MESH,
        )

    def z_copy(e, side, chunk):
        return pltpu.make_async_remote_copy(
            src_ref=fields[e].at[
                pl.ds(1 + chunk * nc, nc), 0 if side == 0 else zts - 1, inside
            ],
            dst_ref=(zhi if side == 0 else zlo).at[e, pl.ds(chunk * nc, nc)],
            send_sem=zs_sem.at[e, side, chunk],
            recv_sem=zr_sem.at[e, 1 - side, chunk],
            device_id=where_to[4 + side],
            device_id_type=MESH,
        )

    tabs = (tab0, tab1, tab2)

    def p_copy(e, k):
        opposite = 1 + (k ^ 1)
        return pltpu.make_async_remote_copy(
            src_ref=tabs[e].at[0] if e < 3 else bucket.at[1 + k],
            dst_ref=tabs[e].at[opposite] if e < 3 else arrived.at[opposite],
            send_sem=ps_sem.at[e, k],
            recv_sem=pr_sem.at[e, k ^ 1],
            device_id=where_to[k],
            device_id_type=MESH,
        )


    def send_faces(e, chunk):
        if chunk == 0:

            @pl.when(there[0])
            def _():
                x_copy(e, 0).start()

        if chunk == CHUNKS - 1:

            @pl.when(there[1])
            def _():
                x_copy(e, 1).start()

        for side in (0, 1):

            @pl.when(there[2 + side])
            def _():
                y_copy(e, side, chunk).start()

            @pl.when(there[4 + side])
            def _():
                z_copy(e, side, chunk).start()

    def await_faces(e, chunk):
        if chunk == 0:

            @pl.when(there[0])
            def _():
                x_copy(e, 1).wait_recv()

        if chunk == CHUNKS - 1:

            @pl.when(there[1])
            def _():
                x_copy(e, 0).wait_recv()

        for side in (0, 1):

            @pl.when(there[2 + side])
            def _():
                y_copy(e, 1 - side, chunk).wait_recv()

            @pl.when(there[4 + side])
            def _():
                z_copy(e, 1 - side, chunk).wait_recv()

    def send_pores(e):
        for k in range(6):

            @pl.when(there[k])
            def _():
                p_copy(e, k).start()

    def await_pores(e):
        for k in range(6):

            @pl.when(there[k])
            def _():
                p_copy(e, k ^ 1).wait_recv()

    for side, (xat, yat, zbuf) in enumerate(((0, TOP - 1, zlo), (nx + 1, TOP + ny, zhi))):

        @pl.when(jnp.logical_not(there[side]))
        def _():
            for field in fields:
                field[xat, :, inside] = jnp.zeros((zts, ny, LANES), jnp.float32)

        @pl.when(jnp.logical_not(there[2 + side]))
        def _():
            def clear_row(i, carry):
                for field in fields:
                    for zt in range(zts):
                        field[i + 1, zt, yat : yat + 1] = jnp.zeros((1, LANES), jnp.float32)
                return carry

            lax.fori_loop(0, nx, clear_row, 0)

        @pl.when(jnp.logical_not(there[4 + side]))
        def _():
            for e in range(5):

                def clear(i, carry):
                    zbuf[e, i] = jnp.zeros((ny, LANES), jnp.float32)
                    return carry

                lax.fori_loop(0, nx, clear, 0)

    for k in range(6):

        @pl.when(jnp.logical_not(there[k]))
        def _():
            for tab in tabs:
                tab[1 + k] = jnp.zeros((2, pores), jnp.float32)
            arrived[1 + k] = jnp.zeros((1, pores), jnp.float32)

    tab0[0] = press_ref[...]

    pl.semaphore_wait(barrier, total)
    send_pores(0)

    s0, s1, s2 = (table_ref[0], table_ref[1], table_ref[2])
    for chunk in ORDER:
        for zt in range(zts):
            load(0, chunk, zt).wait()
            load(1, chunk, zt).wait()

        def conductivity(i, carry):
            kind = lab[i]
            sig[i + 1, :, inside] = cs[i] * jnp.where(
                kind == 0, s0, jnp.where(kind == 1, s1, s2)
            )
            return carry

        lax.fori_loop(chunk * nc, (chunk + 1) * nc, conductivity, 0)
        send_faces(0, chunk)
    for chunk in ORDER:
        for zt in range(zts):
            load(2, chunk, zt).wait()
        send_faces(1, chunk)

    own = (ix * size_y + iy) * size_z + iz
    bits = pores.bit_length() - 1
    lane_bits = LANES.bit_length() - 1

    def place(device, local):
        delta = device - own
        slot = jnp.zeros(delta.shape, jnp.int32)
        for k, step in enumerate(
            (-size_y * size_z, size_y * size_z, -size_z, size_z, -1, 1)
        ):
            slot = jnp.where(delta == step, k + 1, slot)
        return slot, slot * segs + (local >> lane_bits), local & (LANES - 1)

    nbr = nbr_ref[...]
    _, near_key, near_lane = place(nbr >> bits, nbr & (pores - 1))
    site_pore = spore_ref[...]
    site_slot, site_key, site_lane = place(owner_ref[...], site_pore)
    live = live_ref[...].astype(jnp.float32)
    slot_no = lax.broadcasted_iota(jnp.int32, weight_ref.shape, 0)
    masked = jnp.where(slot_no < count_ref[...], weight_ref[...], 0.0)
    wsum = jnp.sum(masked, axis=0, keepdims=True)
    exch = exch_ref[...]
    pore_no = lax.broadcasted_iota(jnp.int32, (pores, LANES), 0)
    site_rows = site_pore.shape[0]
    for r in range(site_rows):
        hit = jnp.where(pore_no == site_pore[r : r + 1], 1.0, 0.0)
        onehot[:, r * LANES : (r + 1) * LANES] = hit.astype(jnp.bfloat16)

    z_no = lax.broadcasted_iota(jnp.int32, (ny, LANES), 1)
    z_first = z_no == 0
    z_last = z_no == LANES - 1
    low_y = pl.ds(TOP - 1, ny)
    high_y = pl.ds(TOP + 1, ny)

    for sweep in range(SWEEPS_E):
        old = fields[1 + sweep]
        last = sweep == SWEEPS_E - 1
        e = 1 + sweep
        for chunk in ORDER:
            if sweep == 0:
                await_faces(0, chunk)
                for zt in range(zts):
                    load(3, chunk, zt).wait()
            await_faces(e, chunk)

            def relax(i, carry):
                tiles = range(zts)
                phi = [old[i + 1, zt, inside] for zt in tiles]
                if sweep == 0:
                    s = [sig[i + 1, zt, inside] for zt in tiles]
                    after = up_z(s, zhi[0, i], z_last)
                    gz = [0.5 * (s[zt] + after[zt]) for zt in tiles]
                    z_low = 0.5 * (zlo[0, i] + pltpu.roll(s[0], LANES - 1, 1))
                    zlo[0, i] = z_low
                    gz_below = down_z(gz, z_low, z_first)
                    g = []
                    for zt in tiles:
                        near = [
                            0.5 * (s[zt] + sig[i, zt, inside]),
                            0.5 * (s[zt] + sig[i + 2, zt, inside]),
                            0.5 * (s[zt] + sig[i + 1, zt, low_y]),
                            0.5 * (s[zt] + sig[i + 1, zt, high_y]),
                        ]
                        denom = REACT + gz[zt] + gz_below[zt]
                        for face in near:
                            denom = denom + face
                        scale = jnp.where(s[zt] > 0.0, 1.0 / denom, 0.0)
                        inv[i, zt] = scale
                        gxf[i, zt] = near[0]
                        gxf[i + 1, zt] = near[1]
                        glow[i, zt] = near[2]
                        gyf[i, zt] = near[3]
                        gzf[i, zt] = gz[zt]
                        g.append((*near, scale))
                else:
                    gz = [gzf[i, zt] for zt in tiles]
                    z_low = zlo[0, i]
                    g = [
                        (gxf[i, zt], gxf[i + 1, zt], glow[i, zt], gyf[i, zt], inv[i, zt])
                        for zt in tiles
                    ]
                after = up_z(phi, zhi[e, i], z_last)
                below = down_z([gz[zt] * phi[zt] for zt in tiles], z_low * zlo[e, i], z_first)
                for zt in tiles:
                    numer = (
                        src[i, zt]
                        + g[zt][0] * old[i, zt, inside]
                        + g[zt][1] * old[i + 2, zt, inside]
                        + g[zt][2] * old[i + 1, zt, low_y]
                        + g[zt][3] * old[i + 1, zt, high_y]
                        + gz[zt] * after[zt]
                        + below[zt]
                    )
                    value = numer * g[zt][4]
                    if last:
                        fin[i, zt] = value
                    else:
                        fields[e + 1][i + 1, zt, inside] = value
                return carry

            lax.fori_loop(chunk * nc, (chunk + 1) * nc, relax, 0)
            if last:
                for zt in range(zts):
                    unload(chunk, zt).start()
            else:
                send_faces(e + 1, chunk)

    y_bits, z_bits = (ny.bit_length() - 1, nz.bit_length() - 1)
    sub = lax.broadcasted_iota(jnp.int32, (8, LANES), 0)
    lane_no = lax.broadcasted_iota(jnp.int32, (1, LANES), 1)

    def spread(a, r):
        return jnp.broadcast_to(a[r : r + 1], (8, LANES))

    def pick(j, volts):
        here = lane_no == j
        picked = []
        for r in range(site_rows):
            v = voxel_ref[r, j]
            row = fin[
                v >> (z_bits + y_bits),
                (v >> lane_bits) & (zts - 1),
                pl.ds((v >> z_bits) & (ny - 1), 1),
            ]
            row = pltpu.roll(row, (j - v) & (LANES - 1), 1)
            picked.append(jnp.where(here, row, volts[r]))
        return tuple(picked)

    zero = jnp.zeros((8, LANES), jnp.float32)
    volts = lax.fori_loop(0, LANES, pick, (zero[0:1],) * site_rows, unroll=4)
    volt = jnp.concatenate(volts, axis=0)
    ratio = tpress_ref[1:2, :] / tpress_ref[0:1, :]
    ratio = jnp.concatenate(
        [ratio[:, r * LANES : (r + 1) * LANES] for r in range(site_rows)], axis=0
    )
    eta = volt - 0.5 * jnp.log(ratio)
    current = live * rate_ref[...] * (jnp.exp(0.6 * eta) - jnp.exp(-0.4 * eta))

    spread_current = jnp.concatenate(
        [
            jnp.where(sub == spread(site_slot, r), spread(current, r), 0.0)
            for r in range(site_rows)
        ],
        axis=1,
    )
    high = spread_current.astype(jnp.bfloat16).astype(jnp.float32)
    rest = spread_current - high
    middle = rest.astype(jnp.bfloat16).astype(jnp.float32)
    low = rest - middle
    parts = jnp.concatenate([high, middle, low, jnp.zeros_like(low)], axis=0).astype(jnp.bfloat16)
    sums = lax.dot_general(
        parts, onehot[...], (((1,), (1,)), ((), ())), preferred_element_type=jnp.float32
    )
    sums = sums[0:8] + sums[8:16] + sums[16:24]
    for k in range(SLOTS):
        bucket[k] = sums[k : k + 1]
    send_pores(3)

    def look_up(tab, key, lane):
        found = [zero, zero]
        for k in range(SLOTS):
            for seg in range(segs):
                hit = key == k * segs + seg
                for c in range(2):
                    row = tab[k, c : c + 1, seg * LANES : (seg + 1) * LANES]
                    got = jnp.take_along_axis(jnp.broadcast_to(row, (8, LANES)), lane, axis=1)
                    found[c] = jnp.where(hit, got, found[c])
        return found

    def diffuse(tab):
        near = ([], [])
        for j in range(segs):
            cut = slice(j * LANES, (j + 1) * LANES)
            a, b = look_up(tab, near_key[:, cut], near_lane[:, cut])
            near[0].append(a)
            near[1].append(b)
        sum_a = jnp.sum(masked * jnp.concatenate(near[0], axis=1), axis=0, keepdims=True)
        sum_b = jnp.sum(masked * jnp.concatenate(near[1], axis=1), axis=0, keepdims=True)
        mag_a = jnp.abs(tab[0, 0:1])
        mag_b = jnp.abs(tab[0, 1:2])
        size = mag_a + mag_b + 1.0
        diff_a = DK_A / (1.0 + DK_A / DIFF_M * mag_b / size)
        diff_b = DK_B / (1.0 + DK_B / DIFF_M * mag_a / size)
        return (
            diff_a * sum_a + exch * BATH_A,
            diff_b * sum_b + exch * BATH_B,
            diff_a * wsum + exch,
            diff_b * wsum + exch,
        )

    await_pores(0)
    drawn = None
    for sweep in range(SWEEPS_G):
        top_a, top_b, bottom_a, bottom_b = diffuse(tabs[sweep])
        if sweep == 0:
            await_pores(3)
            drawn = bucket[0]
            for k in range(6):
                drawn = drawn + arrived[1 + k]
            drawn = CURRENT_SCALE * drawn
        new_a = (top_a - drawn) / bottom_a
        new_b = (top_b + drawn) / bottom_b
        tabs[sweep + 1][0, 0:1] = new_a
        tabs[sweep + 1][0, 1:2] = new_b
        send_pores(sweep + 1)
        if sweep == SWEEPS_G - 1:
            press_out[0:1, :] = new_a
            press_out[1:2, :] = new_b
        await_pores(sweep + 1)

    found = look_up(tabs[SWEEPS_G], site_key, site_lane)
    for c in range(2):
        values = found[c] * live
        for r in range(site_rows):
            tile_out[c : c + 1, r * LANES : (r + 1) * LANES] = values[r : r + 1]

    for e in range(5):
        for side in (0, 1):

            @pl.when(there[side])
            def _():
                x_copy(e, side).wait_send()

            for chunk in range(CHUNKS):

                @pl.when(there[2 + side])
                def _():
                    y_copy(e, side, chunk).wait_send()

                @pl.when(there[4 + side])
                def _():
                    z_copy(e, side, chunk).wait_send()

    for e in range(4):
        for k in range(6):

            @pl.when(there[k])
            def _():
                p_copy(e, k).wait_send()

    for chunk in range(CHUNKS):
        for zt in range(zts):
            unload(chunk, zt).wait()


def body(
    labels,
    conduct_scale,
    phase_sigma,
    source,
    potential_in,
    site_voxel,
    site_owner,
    site_pore,
    site_live,
    site_rate,
    tile_press_in,
    throat_nbr,
    throat_count,
    throat_weight,
    pore_exchange,
    pore_press_in,
):
    sizes = (lax.axis_size("gx"), lax.axis_size("gy"), lax.axis_size("gz"))
    nx, ny, nz = source.shape
    pores = pore_exchange.shape[0]
    sites = site_voxel.shape[0]
    f32 = jnp.float32

    zts = nz // LANES

    def brick(extra=0, kind=f32):
        return pltpu.VMEM((nx + extra, zts, ny, LANES), kind)

    def field():
        return pltpu.VMEM((nx + 2, zts, ny + 2 * TOP, LANES), f32)

    dma = pltpu.SemaphoreType.DMA
    any_spec = pl.BlockSpec(memory_space=pl.ANY)
    vmem = pl.BlockSpec(memory_space=pltpu.VMEM)
    by_row = (sites // LANES, LANES)
    return pl.pallas_call(
        functools.partial(kernel, sizes),
        out_shape=(
            jax.ShapeDtypeStruct((nx, ny, nz), f32),
            jax.ShapeDtypeStruct((2, pores), f32),
            jax.ShapeDtypeStruct((2, sites), f32),
        ),
        in_specs=[pl.BlockSpec(memory_space=pltpu.SMEM)] + [any_spec] * 4
        + [pl.BlockSpec(memory_space=pltpu.SMEM)]
        + [vmem] * 10,
        out_specs=(any_spec, vmem, vmem),
        scratch_shapes=[
            brick(0, jnp.int32),
            brick(),
            brick(),
            field(),
            field(),
            field(),
            field(),
            field(),
            brick(),
            brick(1),
            brick(),
            brick(),
            brick(),
            brick(),
            pltpu.VMEM((5, nx, ny, LANES), f32),
            pltpu.VMEM((5, nx, ny, LANES), f32),
            pltpu.VMEM((pores, sites), jnp.bfloat16),
            pltpu.VMEM((SLOTS, 2, pores), f32),
            pltpu.VMEM((SLOTS, 2, pores), f32),
            pltpu.VMEM((SLOTS, 2, pores), f32),
            pltpu.VMEM((SLOTS, 1, pores), f32),
            pltpu.VMEM((SLOTS, 1, pores), f32),
            dma((4, CHUNKS, zts)),
            dma((CHUNKS, zts)),
            dma((5, 2)),
            dma((5, 2)),
            dma((5, 2, CHUNKS)),
            dma((5, 2, CHUNKS)),
            dma((5, 2, CHUNKS)),
            dma((5, 2, CHUNKS)),
            dma((4, 6)),
            dma((4, 6)),
        ],
        compiler_params=pltpu.CompilerParams(
            collective_id=0, has_side_effects=True, vmem_limit_bytes=58 * 1024 * 1024
        ),
    )(
        phase_sigma,
        labels,
        conduct_scale,
        source,
        potential_in,
        site_voxel.reshape(by_row),
        site_owner.reshape(by_row),
        site_pore.reshape(by_row),
        site_live.reshape(by_row),
        site_rate.reshape(by_row),
        tile_press_in,
        throat_nbr,
        throat_count.reshape(1, pores),
        throat_weight,
        pore_exchange.reshape(1, pores),
        pore_press_in,
    )


def solution(mesh):
    return jax.shard_map(
        body,
        mesh=mesh,
        in_specs=(
            P("gx", "gy", "gz"),
            P("gx", "gy", "gz"),
            P(),
            P("gx", "gy", "gz"),
            P("gx", "gy", "gz"),
            P(("gx", "gy", "gz")),
            P(("gx", "gy", "gz")),
            P(("gx", "gy", "gz")),
            P(("gx", "gy", "gz")),
            P(("gx", "gy", "gz")),
            P(None, ("gx", "gy", "gz")),
            P(None, ("gx", "gy", "gz")),
            P(("gx", "gy", "gz")),
            P(None, ("gx", "gy", "gz")),
            P(("gx", "gy", "gz")),
            P(None, ("gx", "gy", "gz")),
        ),
        out_specs=(P("gx", "gy", "gz"), P(None, ("gx", "gy", "gz")), P(None, ("gx", "gy", "gz"))),
        check_vma=False,
    )
```
